32 devices in a mesh: dp: 8 (over z, y), fsdp: 4 (over x, core).
Axes of the slice: x: 2, y: 2, z: 4, core: 2. Of those that a mesh axis runs over, the one named last changes fastest.
Arguments:
- tokens: bfloat16 [8, 4, 1528, 384], P('dp', 'fsdp'), may hold values from -6 to 6
- focal_count: int32 [8, 4], P('dp', 'fsdp'), may hold values from 0 to 20
- cls_order: int32 [4, 192], P('fsdp', 'dp'), may hold values from 0 to 191, each once within a row
- out_cotangent: bfloat16 [8, 4, 1528, 384], P('dp', 'fsdp'), may hold values from -6 to 6
- cls_cotangent: bfloat16 [8, 4, 24, 384], P('dp', 'fsdp'), may hold values from -6 to 6
- qkv_weight: float32 [2, 384, 1152], P(None, 'dp', 'fsdp'), may hold values from -0.3125 to 0.3125
- proj_weight: float32 [2, 384, 384], P(None, 'dp', 'fsdp'), may hold values from -0.625 to 0.625
- fc1_weight: float32 [2, 384, 1536], P(None, 'dp', 'fsdp'), may hold values from -0.3125 to 0.3125
- fc2_weight: float32 [2, 1536, 384], P(None, 'dp', 'fsdp'), may hold values from -0.15625 to 0.15625
- vec_params: float32 [2, 384, 12], P(None, 'dp', 'fsdp'), may hold values from -1.2 to 1.5, as said below
- qkv_first: float32 [2, 384, 1152], P(None, 'dp', 'fsdp'), may hold values from -640 to 640
- proj_first: float32 [2, 384, 384], P(None, 'dp', 'fsdp'), may hold values from -640 to 640
- fc1_first: float32 [2, 384, 1536], P(None, 'dp', 'fsdp'), may hold values from -640 to 640
- fc2_first: float32 [2, 1536, 384], P(None, 'dp', 'fsdp'), may hold values from -640 to 640
- vec_first: float32 [2, 384, 12], P(None, 'dp', 'fsdp'), may hold values from -640 to 640
- qkv_second: float32 [2, 384, 1152], P(None, 'dp', 'fsdp'), may hold values from 12224 to 48896
- proj_second: float32 [2, 384, 384], P(None, 'dp', 'fsdp'), may hold values from 12224 to 48896
- fc1_second: float32 [2, 384, 1536], P(None, 'dp', 'fsdp'), may hold values from 12224 to 48896
- fc2_second: float32 [2, 1536, 384], P(None, 'dp', 'fsdp'), may hold values from 12224 to 48896
- vec_second: float32 [2, 384, 12], P(None, 'dp', 'fsdp'), may hold values from 12224 to 48896
Outputs:
- activations: bfloat16 [8, 4, 1528, 384], P('dp', 'fsdp')
- cls_regrouped: bfloat16 [8, 4, 24, 384], P('dp', 'fsdp')
- input_grad: float32 [8, 4, 1528, 384], P('dp', 'fsdp')
- qkv_new: float32 [2, 384, 1152], P(None, 'dp', 'fsdp')
- proj_new: float32 [2, 384, 384], P(None, 'dp', 'fsdp')
- fc1_new: float32 [2, 384, 1536], P(None, 'dp', 'fsdp')
- fc2_new: float32 [2, 1536, 384], P(None, 'dp', 'fsdp')
- vec_new: float32 [2, 384, 12], P(None, 'dp', 'fsdp')
- qkv_first_new: float32 [2, 384, 1152], P(None, 'dp', 'fsdp')
- proj_first_new: float32 [2, 384, 384], P(None, 'dp', 'fsdp')
- fc1_first_new: float32 [2, 384, 1536], P(None, 'dp', 'fsdp')
- fc2_first_new: float32 [2, 1536, 384], P(None, 'dp', 'fsdp')
- vec_first_new: float32 [2, 384, 12], P(None, 'dp', 'fsdp')
- qkv_second_new: float32 [2, 384, 1152], P(None, 'dp', 'fsdp')
- proj_second_new: float32 [2, 384, 384], P(None, 'dp', 'fsdp')
- fc1_second_new: float32 [2, 384, 1536], P(None, 'dp', 'fsdp')
- fc2_second_new: float32 [2, 1536, 384], P(None, 'dp', 'fsdp')
- vec_second_new: float32 [2, 384, 12], P(None, 'dp', 'fsdp')
The draws below stay inside these ranges and needn't reach their ends.
Inputs may be any that keep to these rules, and one draw needn't show every extreme that they name: `vec_params`: columns 0 and 2 of each block are gains, the others biases. `cls_order`: each row names every index once.
All inputs are finite; a program needn't handle non-finite values.
Results may differ from the reference program's by a relative error of at most 0.012.
Values may be sent and summed in bfloat16 or wider, within the bound.
A program may use at most 192 MiB of HBM per device.

```python
import math
import jax
import jax.numpy as jnp
from jax import lax

D = 384
HEADS = 6
HEAD_DIM = 64
FF = 1536
GLOB_TOK = 197
CROP_TOK = 37
STEP = 5
VIEWS = 4
CROPS = 20
TOK_DEV = 1528
CLS_DEV = 24
TOKENS = 48896
N_DP = 8
N_FSDP = 4


def draw_vec_params(key, part):
    key = jax.random.fold_in(key, 7)
    gain_key, shift_key = jax.random.split(key)
    gains = jax.random.uniform(gain_key, (2, D, 12), jnp.float32, 0.5, 1.5)
    shifts = jnp.clip(0.3 * jax.random.normal(shift_key, (2, D, 12), jnp.float32), -1.2, 1.2)
    column = jnp.arange(12)
    is_gain = jnp.logical_or(column == 0, column == 2)
    return jnp.where(is_gain[None, None, :], gains, shifts)


def with_ends(drawn, own_key, smallest, largest):
    longest = drawn.shape.index(max(drawn.shape))
    spots = []
    for shift in (0, 1):
        where = [jax.random.randint(jax.random.fold_in(own_key, axis), (), 0, length) for axis, length in enumerate(drawn.shape)]
        where[longest] = (where[longest] + shift) % drawn.shape[longest]
        spots.append(tuple(where))
    return drawn.at[spots[0]].set(smallest).at[spots[1]].set(largest)


def block_scale(rng, dims, cuts, low, largest):
    level, own = 1.0, jax.random.fold_in(rng, 6)
    for dim, shards_of in cuts:
        heights = jnp.exp(jax.random.uniform(jax.random.fold_in(own, dim), (shards_of,), jnp.float32, low / len(cuts), largest / len(cuts)))
        level = level * jnp.repeat(heights, dims[dim] // shards_of).reshape([-1 if axis == dim else 1 for axis in range(len(dims))])
    return level


def normal_values(key, shape, spread, bound, pieces=(), kind=jnp.bfloat16):
    loudness = block_scale(key, shape, pieces, -0.22, 0.18) if pieces else 1.0
    drawn = jax.random.normal(key, shape, jnp.float32) * spread * loudness
    return jnp.minimum(jnp.maximum(drawn, -bound), bound).astype(kind)


def setup_inputs(seed: int = 0) -> dict:
    key_list = jax.random.split(jax.random.key(seed), 21)
    return {
        "tokens": normal_values(key_list[0], (N_DP, N_FSDP, TOK_DEV, D), 1.0, 6.0, ((0, 8), (1, 4))),
        "focal_count": with_ends(jax.random.randint(key_list[1], (N_DP, N_FSDP), 0, CROPS + 1), jax.random.fold_in(key_list[1], 1), 0, CROPS).astype(jnp.int32),
        "cls_order": jax.vmap(lambda own: jax.random.permutation(own, N_DP * CLS_DEV))(jax.random.split(key_list[2], N_FSDP)).reshape((N_FSDP, N_DP * CLS_DEV)).astype(jnp.int32),
        "out_cotangent": normal_values(key_list[3], (N_DP, N_FSDP, TOK_DEV, D), 1.0, 6.0, ((0, 8), (1, 4))),
        "cls_cotangent": normal_values(key_list[4], (N_DP, N_FSDP, CLS_DEV, D), 1.0, 6.0, ((0, 8), (1, 4))),
        "qkv_weight": normal_values(key_list[5], (2, D, 3 * D), D ** -0.5, 0.3125, ((1, 8), (2, 4)), jnp.float32),
        "proj_weight": normal_values(key_list[6], (2, D, D), (D // 4) ** -0.5, 0.625, ((1, 8), (2, 4)), jnp.float32),
        "fc1_weight": normal_values(key_list[7], (2, D, FF), D ** -0.5, 0.3125, ((1, 8), (2, 4)), jnp.float32),
        "fc2_weight": normal_values(key_list[8], (2, FF, D), FF ** -0.5, 0.15625, ((1, 8), (2, 4)), jnp.float32),
        "vec_params": draw_vec_params(jax.random.fold_in(key_list[20], 71), 0),
        "qkv_first": normal_values(key_list[10], (2, D, 3 * D), (0.5 * TOKENS ** 0.5), 640.0, ((1, 8), (2, 4)), jnp.float32),
        "proj_first": normal_values(key_list[11], (2, D, D), (0.5 * TOKENS ** 0.5), 640.0, ((1, 8), (2, 4)), jnp.float32),
        "fc1_first": normal_values(key_list[12], (2, D, FF), (0.5 * TOKENS ** 0.5), 640.0, ((1, 8), (2, 4)), jnp.float32),
        "fc2_first": normal_values(key_list[13], (2, FF, D), (0.5 * TOKENS ** 0.5), 640.0, ((1, 8), (2, 4)), jnp.float32),
        "vec_first": normal_values(key_list[14], (2, D, 12), (0.5 * TOKENS ** 0.5), 640.0, ((1, 8), (2, 4)), jnp.float32),
        "qkv_second": jnp.clip(jnp.exp(math.log(48896.0) - 1.3862944 * jax.random.uniform(key_list[15], (2, D, 3 * D), jnp.float32) ** block_scale(key_list[15], (2, D, 3 * D), ((1, 8), (2, 4)), -0.2, 0.2)), 12224.0, 48896.0),
        "proj_second": jnp.clip(jnp.exp(math.log(48896.0) - 1.3862944 * jax.random.uniform(key_list[16], (2, D, D), jnp.float32) ** block_scale(key_list[16], (2, D, D), ((1, 8), (2, 4)), -0.2, 0.2)), 12224.0, 48896.0),
        "fc1_second": jnp.clip(jnp.exp(math.log(48896.0) - 1.3862944 * jax.random.uniform(key_list[17], (2, D, FF), jnp.float32) ** block_scale(key_list[17], (2, D, FF), ((1, 8), (2, 4)), -0.2, 0.2)), 12224.0, 48896.0),
        "fc2_second": jnp.clip(jnp.exp(math.log(48896.0) - 1.3862944 * jax.random.uniform(key_list[18], (2, FF, D), jnp.float32) ** block_scale(key_list[18], (2, FF, D), ((1, 8), (2, 4)), -0.2, 0.2)), 12224.0, 48896.0),
        "vec_second": jnp.clip(jnp.exp(math.log(48896.0) - 1.3862944 * jax.random.uniform(key_list[19], (2, D, 12), jnp.float32) ** block_scale(key_list[19], (2, D, 12), ((1, 8), (2, 4)), -0.2, 0.2)), 12224.0, 48896.0),
    }


@jax.custom_vjp
def low(v):
    return lax.optimization_barrier(v.astype(jnp.bfloat16)).astype(jnp.float32)

@jax.custom_vjp
def low_back(v):
    return v

def low_keep(v):
    return (low(v), None)

def low_pass(kept, grad):
    return (grad,)

def back_keep(v):
    return (v, None)

def back_low(kept, grad):
    return (low(grad),)
low.defvjp(low_keep, low_pass)
low_back.defvjp(back_keep, back_low)
beta_one = 0.5
beta_two = 0.5
step_rate = 0.03
vector_rate = 0.4
weight_decay = 0.05
adam_epsilon = 1e-08
norm_epsilon = 1e-06
highest = lax.Precision.HIGHEST

def layer_norm(inputs, gain_vector, shift_vector):
    centre = lax.optimization_barrier(jnp.mean(inputs, axis=-1, keepdims=True))
    centred = inputs - centre
    variance = lax.optimization_barrier(jnp.mean(centred * centred, axis=-1, keepdims=True))
    return centred * lax.rsqrt(variance + norm_epsilon) * gain_vector + shift_vector

def product(left_side, right_side):
    return jnp.dot(left_side, right_side, precision=highest, preferred_element_type=jnp.float32)

def attend_group(queries, key_rows, values):
    scores = low_back(HEAD_DIM ** (-0.5) * jnp.einsum('bqhe,bkhe->bhqk', queries, key_rows, precision=highest))
    soft_weights = low(jax.nn.softmax(scores, axis=-1))
    mixed_rows = jnp.einsum('bhqk,bkhe->bqhe', soft_weights, values, precision=highest)
    return low(low_back(mixed_rows))
attend_checked = jax.checkpoint(attend_group)

def attention(queries, key_rows, values):
    boundary = VIEWS * GLOB_TOK
    glob_parts = [member[:boundary].reshape(VIEWS, GLOB_TOK, HEADS, HEAD_DIM) for member in (queries, key_rows, values)]
    crop_parts = [member[boundary:].reshape(CROPS, CROP_TOK, HEADS, HEAD_DIM) for member in (queries, key_rows, values)]
    glob_out = attend_checked(*glob_parts).reshape(boundary, D)
    crop_out = attend_checked(*crop_parts).reshape(CROPS * CROP_TOK, D)
    return jnp.concatenate([glob_out, crop_out], axis=0)

def run_block(tok_rows, layer_params):
    qkv_matrix, proj_matrix, up_matrix, down_matrix, vectors = [low(param) for param in layer_params]
    up_bias = vectors[:, 7:11].T.reshape(FF)
    normed_one = low(layer_norm(tok_rows, vectors[:, 0], vectors[:, 1]))
    projected = low_back(product(normed_one, qkv_matrix))
    queries = low(projected[:, :D] + vectors[:, 4])
    key_rows = low(projected[:, D:2 * D])
    values = low(projected[:, 2 * D:] + vectors[:, 5])
    mixed_rows = attention(queries, key_rows, values)
    attended = tok_rows + (low_back(product(mixed_rows, proj_matrix)) + vectors[:, 6])
    normed_two = low(layer_norm(attended, vectors[:, 2], vectors[:, 3]))
    hidden = low_back(product(normed_two, up_matrix)) + up_bias
    activated = low(jax.nn.gelu(hidden, approximate=False))
    return attended + (low_back(product(activated, down_matrix)) + vectors[:, 11])

def forward(tokens_all, params, focal_count, cls_order):
    devices_all = N_DP * N_FSDP

    def one_device(tok_rows):
        for layer_index in range(2):
            tok_rows = run_block(tok_rows, tuple((param[layer_index] for param in params)))
        return tok_rows
    finals = lax.map(jax.checkpoint(one_device), tokens_all)
    boundary = VIEWS * GLOB_TOK
    positions = jnp.arange(TOK_DEV, dtype=jnp.int32)
    crop_index = (positions - boundary) // CROP_TOK
    counts = focal_count.reshape(devices_all, 1).astype(jnp.int32)
    live_mask = jnp.logical_or(positions[None, :] < boundary, crop_index[None, :] < counts)
    finals = finals * live_mask[:, :, None].astype(finals.dtype)
    starts = jnp.concatenate([jnp.arange(VIEWS, dtype=jnp.int32) * GLOB_TOK, boundary + jnp.arange(CROPS, dtype=jnp.int32) * CROP_TOK])
    class_all = finals[:, starts].reshape(N_DP, N_FSDP, CLS_DEV, D)
    by_column = jnp.transpose(class_all, (1, 0, 2, 3)).reshape(N_FSDP, N_DP * CLS_DEV, D)
    picked = jnp.take_along_axis(by_column, cls_order.astype(jnp.int32)[:, :, None], axis=1)
    regrouped = jnp.transpose(picked.reshape(N_FSDP, N_DP, CLS_DEV, D), (1, 0, 2, 3))
    return (finals, regrouped)

def adamw(weight, first_moment, second, gradient, decay_factor, rate):
    new_first = beta_one * first_moment + (1.0 - beta_one) * gradient
    new_second = beta_two * second + (1.0 - beta_two) * gradient * gradient
    first_hat = new_first / (1.0 - beta_one ** STEP)
    second_hat = new_second / (1.0 - beta_two ** STEP)
    new_weight = weight - rate * (first_hat / (jnp.sqrt(second_hat) + adam_epsilon) + decay_factor * weight_decay * weight)
    return (new_weight, new_first, new_second)

def reference(tokens, focal_count, cls_order, out_cotangent, cls_cotangent, qkv_weight, proj_weight, fc1_weight, fc2_weight, vec_params, qkv_first, proj_first, fc1_first, fc2_first, vec_first, qkv_second, proj_second, fc1_second, fc2_second, vec_second):
    devices_all = N_DP * N_FSDP
    tokens_all = tokens.astype(jnp.float32).reshape(devices_all, TOK_DEV, D)
    params = (qkv_weight, proj_weight, fc1_weight, fc2_weight, vec_params)

    def run_all(inputs, weights):
        return forward(inputs, weights, focal_count, cls_order)
    (finals, regrouped), pull_back = jax.vjp(run_all, tokens_all, params)
    input_part, gradients = pull_back((out_cotangent.astype(jnp.float32).reshape(devices_all, TOK_DEV, D), cls_cotangent.astype(jnp.float32)))
    qkv_new, qkv_first_new, qkv_second_new = adamw(qkv_weight, qkv_first, qkv_second, gradients[0], 1.0, step_rate)
    proj_new, proj_first_new, proj_second_new = adamw(proj_weight, proj_first, proj_second, gradients[1], 1.0, step_rate)
    fc1_new, fc1_first_new, fc1_second_new = adamw(fc1_weight, fc1_first, fc1_second, gradients[2], 1.0, step_rate)
    fc2_new, fc2_first_new, fc2_second_new = adamw(fc2_weight, fc2_first, fc2_second, gradients[3], 1.0, step_rate)
    vec_new, vec_first_new, vec_second_new = adamw(vec_params, vec_first, vec_second, gradients[4], 0.0, vector_rate)
    activations = finals.reshape(N_DP, N_FSDP, TOK_DEV, D).astype(jnp.bfloat16)
    cls_regrouped = regrouped.astype(jnp.bfloat16)
    input_grad = input_part.reshape(N_DP, N_FSDP, TOK_DEV, D)
    return (activations, cls_regrouped, input_grad, qkv_new, proj_new, fc1_new, fc2_new, vec_new, qkv_first_new, proj_first_new, fc1_first_new, fc2_first_new, vec_first_new, qkv_second_new, proj_second_new, fc1_second_new, fc2_second_new, vec_second_new)
```

```python
import jax
import jax.numpy as jnp
import numpy as np
from jax import lax
from jax.experimental import pallas as pl
from jax.experimental.pallas import tpu as pltpu
from jax.sharding import PartitionSpec as P

D = 384
HEADS = 6
HEAD_DIM = 64
FF = 1536
GLOB_TOK = 197
CROP_TOK = 37
STEP = 5
VIEWS = 4
CROPS = 20
CROP_GROUP = 5
GROUPS = CROPS // CROP_GROUP
TILE = 208
TILES = VIEWS + GROUPS
ROWS = TILE * TILES
PER_STEP = 2
CHUNK = TILE * PER_STEP
STEPS = TILES // PER_STEP
CLS_DEV = VIEWS + CROPS
TOK_DEV = VIEWS * GLOB_TOK + CROPS * CROP_TOK
CLS_PAD = 32
SHARD = 48
PACKS = 3
SUB = 64
WIDE_SUB = 64
SLOTS = 3
WIDE = 1552
GATHERED = (2, 2, 4, 2, SHARD, D)
SPLIT = (PACKS, *GATHERED)

beta_one = 0.5
beta_two = 0.5
step_rate = 0.03
vector_rate = 0.4
weight_decay = 0.05
adam_epsilon = 1e-08
norm_epsilon = 1e-06
score_scale = HEAD_DIM ** (-0.5)

BF16 = jnp.bfloat16
F32 = jnp.float32
VMEM_LIMIT = 60 * 1024 * 1024
MESH = pl.DeviceIdType.MESH


def dot(left, right):
    return lax.dot_general(left, right, (((1,), (0,)), ((), ())), preferred_element_type=F32)


def dot_t(left, right):
    return lax.dot_general(left, right, (((1,), (1,)), ((), ())), preferred_element_type=F32)


def normalise(rows):
    centre = jnp.mean(rows, axis=-1, keepdims=True)
    centred = rows - centre
    variance = jnp.mean(centred * centred, axis=-1, keepdims=True)
    spread = lax.rsqrt(variance + norm_epsilon)
    return centred * spread, spread


def norm_back(grad, unit, spread, gain):
    scaled = grad * gain
    return spread * (
        scaled
        - jnp.mean(scaled, axis=-1, keepdims=True)
        - unit * jnp.mean(scaled * unit, axis=-1, keepdims=True)
    )


def gelu_pair(z):
    t = 1.0 / (1.0 + 0.23164189 * jnp.abs(z))
    bell = jnp.exp2(z * z * -0.72134752)
    poly = t * (
        0.127414796 + t * (-0.142248368 + t * (0.7107068705 + t * (-0.7265760135 + t * 0.5307027145)))
    )
    tail = poly * bell
    phi = jnp.where(z >= 0.0, 1.0 - tail, tail)
    return z * phi, phi + z * (bell * 0.3989422804)


def blocks(total, size):
    return [slice(start, min(start + size, total)) for start in range(0, total, size)]


def fold(value):
    return jnp.sum(value.reshape(value.shape[0] // 8, 8, value.shape[1]), axis=0)


def staged(count, stages):
    for turn in range(count + len(stages) - 1):
        for late, stage in enumerate(stages):
            if 0 <= turn - late < count:
                stage(turn - late)


def add_row(vg_ref, row, value, cols=slice(None)):
    vg_ref[row : row + 1, cols] += jnp.sum(value, axis=0, keepdims=True)


def attend_chunk(h_ref, bias_ref, weights, vec_ref, saved, score_ref, put_mid, unit_ref=None):
    wq, wp = weights
    a1_ref, qkv_ref, pt_ref, o_ref = saved
    total = h_ref.shape[0]
    for at in blocks(total, SUB):
        unit = normalise(h_ref[at, :].astype(F32))[0] if unit_ref is None else unit_ref[at, :]
        a1_ref[at, :] = (unit * vec_ref[0:1, :] + vec_ref[1:2, :]).astype(BF16)
    edges = (0, 512, 1024, 1152)
    made = {}

    def project(part):
        made[part] = dot_t(a1_ref[...], wq[edges[part] : edges[part + 1], :])

    def settle(part):
        for lane in range(edges[part], edges[part + 1], 128):
            cols = slice(lane, lane + 128)
            kind, own = lane // D, slice(lane % D, lane % D + 128)
            for at in blocks(total, WIDE_SUB):
                piece = made[part][at, lane - edges[part] : lane - edges[part] + 128]
                if kind == 0:
                    piece = (piece + vec_ref[4:5, own]).astype(BF16) * score_scale
                elif kind == 2:
                    piece = piece + vec_ref[5:6, own]
                qkv_ref[at, cols] = piece.astype(BF16)

    staged(3, (project, settle))

    low_half = lax.broadcasted_iota(jnp.int32, (TILE, 128), 1) < HEAD_DIM
    items = [(tile, pair) for tile in range(total // TILE) for pair in range(HEADS // 2)]

    def score(index):
        tile, pair = items[index]
        at = slice(tile * TILE, (tile + 1) * TILE)
        q = qkv_ref[at, pair * 128 : pair * 128 + 128]
        k = qkv_ref[at, D + pair * 128 : D + pair * 128 + 128]
        zero = jnp.zeros_like(k)
        both = jnp.concatenate([jnp.where(low_half, k, zero), jnp.where(low_half, zero, k)], axis=0)
        score_ref[index % SLOTS] = dot_t(both, q)

    def soften(index):
        tile, pair = items[index]
        for side in range(2):
            head = tile * HEADS + pair * 2 + side
            for half in blocks(TILE, 128):
                piece = score_ref[index % SLOTS, side * TILE : (side + 1) * TILE, half] + bias_ref[0, :, half]
                top = jnp.max(piece, axis=0, keepdims=True)
                raised = jnp.exp(piece - top)
                share = 1.0 / jnp.sum(raised, axis=0, keepdims=True)
                pt_ref[head, :, half] = (raised * share).astype(BF16)

    def mix(index):
        tile, pair = items[index]
        at = slice(tile * TILE, (tile + 1) * TILE)
        vt = qkv_ref[at, 2 * D + pair * 128 : 2 * D + pair * 128 + 128].T
        head = tile * HEADS + pair * 2
        parts = [
            dot(vt[side * HEAD_DIM : (side + 1) * HEAD_DIM, :], pt_ref[head + side]) for side in range(2)
        ]
        o_ref[at, pair * 128 : pair * 128 + 128] = jnp.concatenate(parts, axis=0).T.astype(BF16)

    staged(len(items), (score, soften, mix))
    attended = dot_t(o_ref[...], wp[...])
    for at in blocks(total, SUB):
        h1 = h_ref[at, :].astype(F32) + (attended[at] + vec_ref[6:7, :])
        unit, _ = normalise(h1)
        put_mid(at, h1, (unit * vec_ref[2:3, :] + vec_ref[3:4, :]).astype(BF16))


def expand_chunk(h1_ref, a2_ref, weights, vec_ref, saved, finish):
    w1, w2 = weights
    u_ref, gp_ref = saved
    total = h1_ref.shape[0]
    totals = []
    made = {}

    def up(part):
        made[part] = dot(a2_ref[...], w1[:, part * 256 : (part + 1) * 256])

    def bend(part):
        for lane in range(part * 256, (part + 1) * 256, 128):
            cols, row = slice(lane, lane + 128), 7 + lane // D
            own = slice(lane % D, lane % D + 128)
            for at in blocks(total, WIDE_SUB):
                z = made[part][at, lane - part * 256 : lane - part * 256 + 128] + vec_ref[row : row + 1, own]
                u, slope = gelu_pair(z)
                u_ref[at, cols] = u.astype(BF16)
                gp_ref[at, cols] = slope.astype(BF16)

    def down(part):
        if part % 3 == 2:
            wide = slice((part - 2) * 256, (part + 1) * 256)
            totals.append(dot_t(u_ref[:, wide], w2[:, wide]))

    staged(6, (up, bend, down))
    for at in blocks(total, SUB):
        finish(at, h1_ref[at, :] + (totals[0][at] + totals[1][at] + vec_ref[11:12, :]))


def forward_chunk(h_ref, bias_ref, weights, vec_ref, saved, spare, finish):
    wq, wp, w1, w2 = weights
    a1_ref, qkv_ref, pt_ref, o_ref, h1_ref, a2_ref, u_ref, gp_ref = saved

    def put_mid(at, h1, a2):
        h1_ref[at, :] = h1
        a2_ref[at, :] = a2

    attend_chunk(h_ref, bias_ref, (wq, wp), vec_ref, (a1_ref, qkv_ref, pt_ref, o_ref), spare[0], put_mid)
    expand_chunk(h1_ref, a2_ref, (w1, w2), vec_ref, (u_ref, gp_ref), finish)


def expand_back(dy_at, weights, vec_ref, saved, grads, vg_ref):
    wp, w1, w2 = weights
    h1_ref, gp_ref = saved
    dy_ref, dz_ref, dh_ref, dol_ref, keep_ref = grads
    size = h1_ref.shape[0]
    total = jnp.zeros((8, D), F32)
    for at in blocks(size, SUB):
        dy = dy_at(at)
        dy_ref[at, :] = dy.astype(BF16)
        total = total + fold(dy)
    add_row(vg_ref, 11, total)
    da2 = []
    made = {}

    def up(part):
        made[part] = dot(dy_ref[...], w2[:, part * 256 : (part + 1) * 256])

    def bend(part):
        for lane in range(part * 256, (part + 1) * 256, 128):
            cols = slice(lane, lane + 128)
            for at in blocks(size, WIDE_SUB):
                du = made[part][at, lane - part * 256 : lane - part * 256 + 128]
                dz_ref[at, cols] = (du * gp_ref[at, cols].astype(F32)).astype(BF16)

    def down(part):
        if part % 3 == 2:
            wide = slice((part - 2) * 256, (part + 1) * 256)
            da2.append(dot_t(dz_ref[:, wide], w1[:, wide]))

    staged(6, (up, bend, down))
    totals = [jnp.zeros((8, D), F32) for _ in range(2)]
    for at in blocks(size, SUB):
        unit, spread = normalise(h1_ref[at, :])
        grad = da2[0][at] + da2[1][at]
        dh1 = dy_at(at) + norm_back(grad, unit, spread, vec_ref[2:3, :])
        keep_ref[at, :] = dh1
        dh_ref[at, :] = dh1.astype(BF16)
        totals = [old + fold(new) for old, new in zip(totals, (grad * unit, grad))]
    add_row(vg_ref, 2, totals[0])
    add_row(vg_ref, 3, totals[1])
    dol_ref[...] = dot(dh_ref[...], wp[...]).astype(BF16)


def attend_back(saved, grads, spare):
    qkv_ref, pt_ref, o_ref = saved
    dol_ref, dl_ref = grads
    score_ref, ds_ref = spare
    low_half = lax.broadcasted_iota(jnp.int32, (TILE, 128), 1) < HEAD_DIM
    items = [(tile, pair) for tile in range(qkv_ref.shape[0] // TILE) for pair in range(HEADS // 2)]

    def spread_probs(index):
        tile, pair = items[index]
        at = slice(tile * TILE, (tile + 1) * TILE)
        here = slice(pair * 128, pair * 128 + 128)
        v = qkv_ref[at, 2 * D + pair * 128 : 2 * D + pair * 128 + 128]
        dol = dol_ref[at, here]
        zero = jnp.zeros_like(v)
        both = jnp.concatenate([jnp.where(low_half, v, zero), jnp.where(low_half, zero, v)], axis=0)
        score_ref[index % SLOTS] = dot_t(both, dol)
        head = tile * HEADS + pair * 2
        dv = dot(pt_ref[head : head + 2].reshape(2 * TILE, TILE), dol)
        dv = jnp.where(low_half, dv[:TILE], dv[TILE:])
        dl_ref[at, 2 * D + pair * 128 : 2 * D + pair * 128 + 128] = dv.astype(BF16)

    lane = jnp.where(lax.broadcasted_iota(jnp.int32, (16, 128), 1) < HEAD_DIM, 0, 1)
    pick = jnp.where(lane == lax.broadcasted_iota(jnp.int32, (16, 128), 0), 1.0, 0.0).astype(BF16)

    def through_softmax(index):
        tile, pair = items[index]
        at = slice(tile * TILE, (tile + 1) * TILE)
        here = slice(pair * 128, pair * 128 + 128)
        means = dot_t(pick, o_ref[at, here] * dol_ref[at, here])
        for side in range(2):
            rows = slice(side * TILE, (side + 1) * TILE)
            for half in blocks(TILE, 128):
                wide = pt_ref[tile * HEADS + pair * 2 + side, :, half].astype(F32)
                piece = score_ref[index % SLOTS, rows, half] - means[side : side + 1, half]
                ds_ref[index % SLOTS, rows, half] = (wide * piece).astype(BF16)

    def to_inputs(index):
        tile, pair = items[index]
        at = slice(tile * TILE, (tile + 1) * TILE)
        here = slice(pair * 128, pair * 128 + 128)
        q = qkv_ref[at, here]
        kt = qkv_ref[at, D + pair * 128 : D + pair * 128 + 128].T
        dk = dot(ds_ref[index % SLOTS], q)
        dl_ref[at, D + pair * 128 : D + pair * 128 + 128] = jnp.where(low_half, dk[:TILE], dk[TILE:]).astype(BF16)
        dqt = [
            dot(
                kt[side * HEAD_DIM : (side + 1) * HEAD_DIM, :],
                ds_ref[index % SLOTS, side * TILE : (side + 1) * TILE, :],
            )
            for side in range(2)
        ]
        dl_ref[at, here] = (jnp.concatenate(dqt, axis=0) * score_scale).astype(BF16).T

    staged(len(items), (spread_probs, through_softmax, to_inputs))


def input_back(h_ref, wq, vec_ref, grads, vg_ref, dx_put):
    dl_ref, keep_ref = grads
    da1 = dot(dl_ref[...], wq[...])
    totals = [jnp.zeros((8, D), F32) for _ in range(2)]
    for at in blocks(h_ref.shape[0], SUB):
        unit, spread = normalise(h_ref[at, :].astype(F32))
        grad = da1[at]
        dx_put(at, keep_ref[at, :] + norm_back(grad, unit, spread, vec_ref[0:1, :]))
        totals = [old + fold(new) for old, new in zip(totals, (grad * unit, grad))]
    add_row(vg_ref, 0, totals[0])
    add_row(vg_ref, 1, totals[1])


def backward_chunk(dy_at, h_ref, weights, vec_ref, saved, grads, spare, vg_ref, dx_put):
    wq, wp, w1, w2 = weights
    qkv_ref, pt_ref, o_ref, h1_ref, gp_ref = saved
    dy_ref, dz_ref, dh_ref, dol_ref, dl_ref, keep_ref = grads
    early = (dy_ref, dz_ref, dh_ref, dol_ref, keep_ref)
    expand_back(dy_at, (wp, w1, w2), vec_ref, (h1_ref, gp_ref), early, vg_ref)
    attend_back((qkv_ref, pt_ref, o_ref), (dol_ref, dl_ref), spare)
    input_back(h_ref, wq, vec_ref, (dl_ref, keep_ref), vg_ref, dx_put)


def pick_halves(first, second, width):
    lane = lax.broadcasted_iota(jnp.int32, first.shape, 1)
    return jnp.where(lane < width, first, second)


ONES = 16


def turn_rows(source, turned):
    for part in range(ROWS // 128):
        here = slice(part * 128, part * 128 + 128)
        turned[0:D, here] = source[here, :].T
        turned[D:, here] = jnp.ones((ONES, 128), BF16)


def put_pack(slab_ref, kind, f, value):
    slab_ref[kind, f // 2, f % 2] = value.astype(BF16).reshape(4, 2, SHARD, D)


def down_grads(dy_s, u_s, turned, slab_ref):
    turn_rows(dy_s, turned)
    made = {}

    def multiply(part):
        made[part] = dot(turned[0:D], u_s[:, part * 2 * D : (part + 1) * 2 * D])

    def pack(part):
        for half in range(2):
            couple = 2 * part + half
            grad = made[part][:, half * D : (half + 1) * D]
            for f in range(4):
                top = grad[f * 96 : f * 96 + 48, :]
                bottom = grad[f * 96 + 48 : f * 96 + 96, :]
                even = pick_halves(top, pltpu.roll(bottom, 192, 1), 192)
                odd = pick_halves(pltpu.roll(top, 192, 1), bottom, 192)
                slab_ref[2, f // 2, f % 2, couple, 0] = even.astype(BF16)
                slab_ref[2, f // 2, f % 2, couple, 1] = odd.astype(BF16)

    staged(2, (multiply, pack))


def up_grads(a2_s, dz_s, turned, slab_ref, vg_ref):
    turn_rows(a2_s, turned)
    made = {}

    def multiply(part):
        made[part] = dot(turned[...], dz_s[:, part * 2 * D : (part + 1) * 2 * D])

    def pack(part):
        for half in range(2):
            f = 2 * part + half
            grad = made[part][:, half * D : (half + 1) * D]
            put_pack(slab_ref, 1, f, grad[0:D])
            vg_ref[7 + f : 8 + f, :] = grad[D : D + 1]

    staged(2, (multiply, pack))


def attention_grads(a1_s, dl_s, o_s, dh_s, turned, slab_ref, vg_ref):
    turn_rows(o_s, turned)
    proj = dot(turned[...], dh_s[...])
    vg_ref[6:7, :] = proj[D : D + 1]
    proj = proj[0:D]
    turn_rows(a1_s, turned)
    both = dot(turned[...], dl_s[:, 0 : 2 * D])
    third = dot(turned[...], dl_s[:, 2 * D : 3 * D])
    first, second = both[0:D, 0:D], both[0:D, D : 2 * D]
    vg_ref[4:5, :] = both[D : D + 1, 0:D]
    put_pack(slab_ref, 0, 0, pick_halves(first, pltpu.roll(proj, 288, 1), 288))
    mixed = pick_halves(pltpu.roll(first, 96, 1), pltpu.roll(second, 96, 1), 96)
    put_pack(slab_ref, 0, 1, pick_halves(mixed, pltpu.roll(proj, 192, 1), 288))
    vg_ref[5:6, :] = third[D : D + 1]
    third = third[0:D]
    mixed = pick_halves(pltpu.roll(second, 192, 1), pltpu.roll(third, 192, 1), 192)
    put_pack(slab_ref, 0, 2, pick_halves(mixed, pltpu.roll(proj, 96, 1), 288))
    put_pack(slab_ref, 0, 3, pick_halves(pltpu.roll(third, 288, 1), proj, 288))


def weight_grads(a1_s, dl_s, o_s, dh_s, a2_s, dz_s, u_s, dy_s, turned, slab_ref, vg_ref):
    down_grads(dy_s, u_s, turned, slab_ref)
    up_grads(a2_s, dz_s, turned, slab_ref, vg_ref)
    attention_grads(a1_s, dl_s, o_s, dh_s, turned, slab_ref, vg_ref)


def rows_block(width, dtype=None):
    return pl.BlockSpec((CHUNK, width), lambda i: (i, 0))


def whole(shape):
    return pl.BlockSpec(shape, lambda i: (0,) * len(shape), pipeline_mode=pl.Buffered(1))


WEIGHT_SPECS = [whole((3 * D, D)), whole((D, D)), whole((D, FF)), whole((D, FF)), whole((16, D))]
BIAS_SPEC = pl.BlockSpec((1, TILE, TILE), lambda i: ((i * PER_STEP) // VIEWS, 0, 0))
PT_SPEC = pl.BlockSpec((PER_STEP * HEADS, TILE, TILE), lambda i: (i, 0, 0))
PARAMS = pltpu.CompilerParams(dimension_semantics=("arbitrary",), vmem_limit_bytes=VMEM_LIMIT)


SPARE = [pltpu.VMEM((SLOTS, 2 * TILE, TILE), F32), pltpu.VMEM((SLOTS, 2 * TILE, TILE), BF16)]


def sequence_start(tile):
    if tile < VIEWS:
        return tile * GLOB_TOK, GLOB_TOK
    group = CROP_GROUP * CROP_TOK
    return VIEWS * GLOB_TOK + (tile - VIEWS) * group, group


def untile(step, source, target):
    per_step = source.shape[0] // TILE
    for turn in range(TILES // per_step):

        @pl.when(step == turn)
        def _():
            for tile in range(per_step):
                start, size = sequence_start(turn * per_step + tile)
                target[start : start + size, :] = source[tile * TILE : tile * TILE + size, :]


def first_forward(rows, bias, weights, vec):
    def kernel(x_ref, bias_ref, wq, wp, w1, w2, vec_ref, out_ref, *rest):
        saved, score_ref = rest[:8], rest[8]

        def finish(at, rows):
            out_ref[at, :] = rows

        forward_chunk(x_ref, bias_ref, (wq, wp, w1, w2), vec_ref, saved, (score_ref,), finish)

    shapes = [
        ((ROWS, D), F32, rows_block(D)),
        ((ROWS, D), BF16, rows_block(D)),
        ((ROWS, 3 * D), BF16, rows_block(3 * D)),
        ((TILES * HEADS, TILE, TILE), BF16, PT_SPEC),
        ((ROWS, D), BF16, rows_block(D)),
        ((ROWS, D), F32, rows_block(D)),
        ((ROWS, D), BF16, rows_block(D)),
        ((ROWS, FF), BF16, rows_block(FF)),
        ((ROWS, FF), BF16, rows_block(FF)),
    ]
    outs = pl.pallas_call(
        kernel,
        grid=(STEPS,),
        in_specs=[rows_block(D), BIAS_SPEC] + WEIGHT_SPECS,
        out_specs=[spec for _, _, spec in shapes],
        out_shape=[jax.ShapeDtypeStruct(shape, dtype) for shape, dtype, _ in shapes],
        scratch_shapes=SPARE[:1],
        compiler_params=PARAMS,
        name="first_forward",
    )(rows, bias, *weights, vec)
    return outs[0], outs[1:]


def row_facts(step, count, per_step):
    row = lax.broadcasted_iota(jnp.int32, (per_step * TILE, 1), 0)
    tile = jnp.zeros_like(row)
    for edge in range(1, per_step):
        tile = tile + jnp.where(row >= edge * TILE, 1, 0)
    local = row - tile * TILE
    tile = tile + step * per_step
    crop = jnp.zeros_like(row)
    for edge in range(1, CROP_GROUP):
        crop = crop + jnp.where(local >= edge * CROP_TOK, 1, 0)
    start = local == crop * CROP_TOK
    crop_id = (tile - VIEWS) * CROP_GROUP + crop
    is_glob = tile < VIEWS
    glob_live = jnp.where(local < GLOB_TOK, 1, 0)
    crop_live = jnp.where(local < CROP_GROUP * CROP_TOK, 1, 0) * jnp.where(crop_id < count, 1, 0)
    live = jnp.where(is_glob, glob_live, crop_live)
    glob_cls = jnp.where(local == 0, tile, -1)
    crop_cls = jnp.where(start, crop_id + VIEWS, -1)
    return live, jnp.where(is_glob, glob_cls, crop_cls)


def second_block(rows, bias, weights, vec, cotangent, returned, count):
    per_step = 1
    chunk, steps = per_step * TILE, TILES // per_step

    def chunk_block(width):
        return pl.BlockSpec((chunk, width), lambda i: (i, 0))

    def kernel(
        count_ref, h_ref, cot_ref, ret_ref, bias_ref, wq, wp, w1, w2, vec_ref,
        act_ref, cls_ref, dx_ref, slab_ref, vg_ref,
        a1_s, qkv_s, pt_s, o_s, h1_s, a2_s, u_s, gp_s, dy_s, dz_s, dh_s, dol_s, dl_s, turned, cls_s, dy_in, keep_s, act_s, wide_s, *spare,
    ):
        step = pl.program_id(0)
        here = pl.ds(pl.multiple_of(step * chunk, chunk), chunk)

        @pl.when(step == 0)
        def _():
            vg_ref[...] = jnp.zeros_like(vg_ref)
            cls_s[...] = jnp.zeros_like(cls_s)

        weights = (wq, wp, w1, w2)
        live, cls_id = row_facts(step, count_ref[0, 0], per_step)
        alive = live.astype(F32)
        spot = lax.broadcasted_iota(jnp.int32, (chunk, CLS_PAD), 1) == cls_id
        spot = jnp.where(spot, 1.0, 0.0).astype(BF16)
        extra = dot(spot, ret_ref[...])
        for at in blocks(chunk, SUB):
            dy_in[at, :] = (cot_ref[at, :].astype(F32) + extra[at]) * alive[at]

        def finish(at, rows):
            rows = rows * alive[at]
            act_s[at, :] = rows

        saved = (a1_s.at[here], qkv_s, pt_s, o_s.at[here], h1_s, a2_s.at[here], u_s.at[here], gp_s)
        forward_chunk(h_ref, bias_ref, weights, vec_ref, saved, spare, finish)
        cls_s[...] += lax.dot_general(
            spot, act_s[...].astype(BF16), (((0,), (0,)), ((), ())), preferred_element_type=F32
        )
        untile(step, act_s, wide_s)
        grads = (dy_s.at[here], dz_s.at[here], dh_s.at[here], dol_s, dl_s.at[here], keep_s)

        def dx_put(at, rows):
            dx_ref[at, :] = rows

        backward_chunk(
            lambda at: dy_in[at, :], h_ref, weights, vec_ref, (qkv_s, pt_s, o_s.at[here], h1_s, gp_s), grads, spare,
            vg_ref, dx_put,
        )

        @pl.when(step == steps - 1)
        def _():
            cls_ref[...] = cls_s[...].astype(BF16)
            act_ref[...] = wide_s[...].astype(BF16)
            weight_grads(a1_s, dl_s, o_s, dh_s, a2_s, dz_s, u_s, dy_s, turned, slab_ref, vg_ref)

    return pl.pallas_call(
        kernel,
        grid=(steps,),
        in_specs=[
            pl.BlockSpec(memory_space=pltpu.SMEM),
            chunk_block(D),
            chunk_block(D),
            whole((CLS_PAD, D)),
            pl.BlockSpec((1, TILE, TILE), lambda i: (i * per_step // VIEWS, 0, 0)),
        ]
        + WEIGHT_SPECS,
        out_specs=[
            whole((TOK_DEV, D)),
            whole((CLS_PAD, D)),
            chunk_block(D),
            whole(SPLIT),
            whole((16, D)),
        ],
        out_shape=[
            jax.ShapeDtypeStruct((TOK_DEV, D), BF16),
            jax.ShapeDtypeStruct((CLS_PAD, D), BF16),
            jax.ShapeDtypeStruct((ROWS, D), F32),
            jax.ShapeDtypeStruct(SPLIT, BF16),
            jax.ShapeDtypeStruct((16, D), F32),
        ],
        scratch_shapes=[
            pltpu.VMEM((ROWS, D), BF16),
            pltpu.VMEM((chunk, 3 * D), BF16),
            pltpu.VMEM((per_step * HEADS, TILE, TILE), BF16),
            pltpu.VMEM((ROWS, D), BF16),
            pltpu.VMEM((chunk, D), F32),
            pltpu.VMEM((ROWS, D), BF16),
            pltpu.VMEM((ROWS, FF), BF16),
            pltpu.VMEM((chunk, FF), BF16),
            pltpu.VMEM((ROWS, D), BF16),
            pltpu.VMEM((ROWS, FF), BF16),
            pltpu.VMEM((ROWS, D), BF16),
            pltpu.VMEM((chunk, D), BF16),
            pltpu.VMEM((ROWS, 3 * D), BF16),
            pltpu.VMEM((D + ONES, ROWS), BF16),
            pltpu.VMEM((CLS_PAD, D), F32),
            pltpu.VMEM((chunk, D), F32),
            pltpu.VMEM((chunk, D), F32),
            pltpu.VMEM((chunk, D), F32),
            pltpu.VMEM((TOK_DEV, D), F32),
        ]
        + SPARE,
        compiler_params=PARAMS,
        name="second_block",
    )(count, rows, cotangent, returned, bias, *weights, vec)


def first_backward(dy, rows, saved, weights, vec):
    def kernel(
        dy_ref, x_ref, a1_hbm, qkv_ref, pt_ref, o_ref, h1_ref, a2_hbm, u_hbm, gp_ref, wq, wp, w1, w2, vec_ref,
        dx_ref, slab_ref, vg_ref,
        a1_s, o_s, a2_s, u_s, dy_s, dz_s, dh_s, dol_s, dl_s, turned, keep_s, dx_s, load_sem, *spare,
    ):
        moves = ((a1_hbm, a1_s), (a2_hbm, a2_s), (u_hbm, u_s))
        loads = [pltpu.make_async_copy(there, mine, load_sem.at[i]) for i, (there, mine) in enumerate(moves)]
        step = pl.program_id(0)
        here = pl.ds(pl.multiple_of(step * CHUNK, CHUNK), CHUNK)

        @pl.when(step == 0)
        def _():
            vg_ref[...] = jnp.zeros_like(vg_ref)
            for load in loads:
                load.start()

        o_s[here] = o_ref[...]
        grads = (dy_s.at[here], dz_s.at[here], dh_s.at[here], dol_s, dl_s.at[here], keep_s)

        def dx_put(at, rows):
            dx_s[at, :] = rows

        backward_chunk(
            lambda at: dy_ref[at, :], x_ref, (wq, wp, w1, w2), vec_ref,
            (qkv_ref, pt_ref, o_ref, h1_ref, gp_ref), grads, spare, vg_ref, dx_put,
        )
        untile(step, dx_s, dx_ref)

        @pl.when(step == STEPS - 1)
        def _():
            for load in loads:
                load.wait()
            weight_grads(a1_s, dl_s, o_s, dh_s, a2_s, dz_s, u_s, dy_s, turned, slab_ref, vg_ref)

    there = pl.BlockSpec(memory_space=pl.ANY)
    return pl.pallas_call(
        kernel,
        grid=(STEPS,),
        in_specs=[
            rows_block(D),
            rows_block(D),
            there,
            rows_block(3 * D),
            PT_SPEC,
            rows_block(D),
            rows_block(D),
            there,
            there,
            rows_block(FF),
        ]
        + WEIGHT_SPECS,
        out_specs=[whole((TOK_DEV, D)), whole(SPLIT), whole((16, D))],
        out_shape=[
            jax.ShapeDtypeStruct((TOK_DEV, D), F32),
            jax.ShapeDtypeStruct(SPLIT, BF16),
            jax.ShapeDtypeStruct((16, D), F32),
        ],
        scratch_shapes=[
            pltpu.VMEM((ROWS, D), BF16),
            pltpu.VMEM((ROWS, D), BF16),
            pltpu.VMEM((ROWS, D), BF16),
            pltpu.VMEM((ROWS, FF), BF16),
            pltpu.VMEM((ROWS, D), BF16),
            pltpu.VMEM((ROWS, FF), BF16),
            pltpu.VMEM((ROWS, D), BF16),
            pltpu.VMEM((CHUNK, D), BF16),
            pltpu.VMEM((ROWS, 3 * D), BF16),
            pltpu.VMEM((D + ONES, ROWS), BF16),
            pltpu.VMEM((CHUNK, D), F32),
            pltpu.VMEM((CHUNK, D), F32),
            pltpu.SemaphoreType.DMA((4,)),
        ]
        + SPARE,
        compiler_params=PARAMS,
        name="first_backward",
    )(dy, rows, *saved, *weights, vec)


def adamw(weight, first_moment, second, gradient, decay_factor, rate):
    new_first = beta_one * first_moment + (1.0 - beta_one) * gradient
    new_second = beta_two * second + (1.0 - beta_two) * gradient * gradient
    first_hat = new_first / (1.0 - beta_one**STEP)
    second_hat = new_second / (1.0 - beta_two**STEP)
    new_weight = weight - rate * (
        first_hat / (jnp.sqrt(second_hat) + adam_epsilon) + decay_factor * weight_decay * weight
    )
    return (new_weight, new_first, new_second)


class Place:
    def __init__(self):
        dp, fsdp = lax.axis_index("dp"), lax.axis_index("fsdp")
        self.dp, self.fsdp = dp, fsdp
        self.z, self.y = dp // 2, dp % 2
        self.x, self.core = fsdp // 2, fsdp % 2

    def along_z(self, step):
        return (lax.rem(self.z + step, 4) * 2 + self.y, self.fsdp)

    def in_plane(self, step):
        x, y = self.plane_spot(step)
        return (self.z * 2 + y, x * 2 + self.core)

    def plane_spot(self, step):
        x = 1 - self.x if step & 1 else self.x
        y = 1 - self.y if step & 2 else self.y
        return x, y

    def along_x(self):
        return (self.dp, (1 - self.x) * 2 + self.core)

    def along_y(self):
        return (self.z * 2 + 1 - self.y, self.fsdp)

    def diagonal(self):
        return (self.z * 2 + 1 - self.y, (1 - self.x) * 2 + self.core)

    def sibling(self):
        return (self.dp, self.x * 2 + 1 - self.core)

    def along_dp(self, step):
        return (lax.rem(self.dp + step, 8), self.fsdp)


def greet(place, along_dp=False):
    barrier = pltpu.get_barrier_semaphore()
    if along_dp:
        others = [place.along_dp(step) for step in range(1, 8)]
        others += [place.in_plane(1), place.in_plane(3), place.sibling()]
    else:
        others = [place.along_z(step) for step in (1, 2, 3)]
        others += [place.in_plane(step) for step in (1, 2, 3)] + [place.sibling()]
    for other in others:
        pl.semaphore_signal(barrier, inc=1, device_id=other, device_id_type=MESH)
    pl.semaphore_wait(barrier, len(others))


def remote(source, target, send_sem, recv_sem, device):
    return pltpu.make_async_remote_copy(
        src_ref=source,
        dst_ref=target,
        send_sem=send_sem,
        recv_sem=recv_sem,
        device_id=device,
        device_id_type=MESH,
    )


class Gather:
    def __init__(self, place, items):
        self.place, self.items = place, items

    def copies(self, index, phase):
        place = self.place
        x, core, z, y = place.x, place.core, place.z, place.y
        buf, out_sem, in_sem, short = self.items[index]
        mine = buf.at[x, core, :, y]
        if phase == 0:
            first, plan = 0, [(buf.at[x, core, z, y], place.along_z(s)) for s in (1, 2, 3)]
        elif phase == 1:
            first, plan = 3, [(mine, place.along_x()), (mine, place.along_y())]
            if short:
                plan.append((mine, place.diagonal()))
        elif phase == 2 and not short:
            first = 5
            plan = [(buf.at[1 - x, core, 0:2, y], place.along_y()), (buf.at[x, core, 2:4, 1 - y], place.along_x())]
        else:
            first, plan = 7, [(buf.at[:, core], place.sibling())]
        return [
            remote(part, part, out_sem.at[first + i], in_sem.at[first + i], other)
            for i, (part, other) in enumerate(plan)
        ]

    def arrivals(self, index, phase):
        place = self.place
        x, core, z, y = place.x, place.core, place.z, place.y
        buf, out_sem, in_sem, short = self.items[index]
        if phase == 0:
            first, spots = 0, [buf.at[x, core, lax.rem(z + 4 - s, 4), y] for s in (1, 2, 3)]
        elif phase == 1:
            first, spots = 3, [buf.at[1 - x, core, :, y], buf.at[x, core, :, 1 - y]]
            if short:
                spots.append(buf.at[1 - x, core, :, 1 - y])
        elif phase == 2 and not short:
            first, spots = 5, [buf.at[1 - x, core, 0:2, 1 - y], buf.at[1 - x, core, 2:4, 1 - y]]
        else:
            first, spots = 7, [buf.at[:, 1 - core]]
        return [
            remote(t, t, out_sem.at[first + i], in_sem.at[first + i], place.sibling()) for i, t in enumerate(spots)
        ]

    def phases(self, index):
        return 3 if self.items[index][3] else 4

    def finish(self, index):
        self.wait(index, self.phases(index) - 1)

    def start(self, index, phase):
        for copy in self.copies(index, phase):
            copy.start()

    def wait(self, index, phase):
        for copy in self.arrivals(index, phase):
            copy.wait_recv()

    def step(self, index, phase):
        self.wait(index, phase)
        self.start(index, phase + 1)

    def drain(self):
        for index in range(len(self.items)):
            for phase in range(self.phases(index)):
                for copy in self.copies(index, phase):
                    copy.wait_send()


def assemble(slabs, kind, targets):
    wq, wp, w1, w2 = targets
    for f in range(4):
        slab = slabs[f // 2, f % 2].reshape(D, D)
        if kind == 0:
            turned = slab.T
            wq[f * 288 : (f + 1) * 288, :] = turned[0:288]
            wp[f * 96 : (f + 1) * 96, :] = turned[288:384]
        elif kind == 1:
            w1[:, f * D : (f + 1) * D] = slab
        else:
            for couple in range(4):
                even = slab[couple * 96 : couple * 96 + 48].astype(F32)
                odd = slab[couple * 96 + 48 : couple * 96 + 96].astype(F32)
                top = pick_halves(even, pltpu.roll(odd, 192, 1), 192)
                bottom = pick_halves(pltpu.roll(even, 192, 1), odd, 192)
                cols = slice(couple * D, (couple + 1) * D)
                w2[f * 96 : f * 96 + 48, cols] = top.astype(BF16)
                w2[f * 96 + 48 : f * 96 + 96, cols] = bottom.astype(BF16)


def late_block(shape, first):
    rest = (0,) * (len(shape) - 1)
    return pl.BlockSpec(shape, lambda i: (jnp.clip(i - first, 0, STEPS - 1), *rest))


def gather_forward(qkv, proj, fc1, fc2, vec, order, cot, tokens, out_cot, bias):
    attend_first, expand_first = 1, 1 + STEPS
    last = 2 * STEPS

    def kernel(
        qkv_ref, proj_ref, fc1_ref, fc2_ref, vec_ref, order_ref, cot_ref, bias_ref, tok_hbm, outc_hbm,
        mid_ref, a1_ref, qkvo_ref, pt_ref, o_ref, h1_ref, a2_ref, u_ref, gp_ref, v0_ref, v1_ref, ret_ref,
        rows_hbm, cot_hbm, wq0_hbm, wp0_hbm, w10_hbm, w20_hbm, wq1_hbm, wp1_hbm, w11_hbm, w21_hbm,
        slabs, vslab, wq, wp, w1, w2, stage, out_cls, in_cls, raw, wide, rows_s, cot_s, h1_s, a2_s, score_s,
        send, recv, vsend, vrecv, csend, crecv, rsem, wsem,
    ):
        step = pl.program_id(0)
        place = Place()
        x, core, z, y = place.x, place.core, place.z, place.y
        items = [(slabs.at[c], send.at[c], recv.at[c], c == 0) for c in range(2 * PACKS)]
        items.insert(0, (vslab, vsend, vrecv, True))
        gather = Gather(place, items)
        loads = [
            pltpu.make_async_copy(tok_hbm.at[0, 0], raw.at[0], rsem.at[0]),
            pltpu.make_async_copy(outc_hbm.at[0, 0], raw.at[1], rsem.at[1]),
        ]
        stores = [
            pltpu.make_async_copy(rows_s, rows_hbm, rsem.at[2]),
            pltpu.make_async_copy(cot_s, cot_hbm, rsem.at[3]),
        ]
        weights = (wq, wp, w1, w2)
        keeps = [
            [
                pltpu.make_async_copy(mine.at[block], there, wsem.at[block, i])
                for i, (mine, there) in enumerate(zip(weights, theirs))
            ]
            for block, theirs in enumerate(
                ((wq0_hbm, wp0_hbm, w10_hbm, w20_hbm), (wq1_hbm, wp1_hbm, w11_hbm, w21_hbm))
            )
        ]
        cls = [
            remote(out_cls.at[s], in_cls.at[s - 1], csend.at[s - 1], crecv.at[s - 1], place.along_dp(s))
            for s in range(1, 8)
        ]

        def pack(block):
            stage[0, :, 0:288] = qkv_ref[block]
            stage[1, :, 0:96] = proj_ref[block]
            first = pick_halves(stage[0], pltpu.roll(stage[1], 288, 1), 288).astype(BF16)
            slabs[block * PACKS, x, core, z, y] = first
            slabs[block * PACKS + 1, x, core, z, y] = fc1_ref[block].astype(BF16)
            turned = fc2_ref[block].T
            stage[0, :, 0:192] = turned[0:48]
            stage[1, :, 0:192] = turned[48:96]
            third = pick_halves(stage[0], pltpu.roll(stage[1], 192, 1), 192).astype(BF16)
            slabs[block * PACKS + 2, x, core, z, y] = third

        def tile_rows(source, target):
            loads[source].wait()
            wide[:TOK_DEV] = raw[source].astype(F32)
            for tile in range(TILES):
                first, _ = sequence_start(tile)
                target[tile * TILE : (tile + 1) * TILE, :] = wide[first : first + TILE, :].astype(BF16)
            stores[source].start()

        def land(index):
            gather.finish(index)
            block, kind = (index - 1) // PACKS, (index - 1) % PACKS
            assemble(slabs.at[index - 1], kind, [w.at[block] for w in weights])
            for i in ((0, 1), (2,), (3,))[kind]:
                keeps[block][i].start()

        @pl.when(step == 0)
        def _():
            for load in loads:
                load.start()
            pack(0)
            stage[0, :, 0:128] = jnp.zeros((SHARD, 128), F32)
            stage[1, :, 0:128] = jnp.zeros((SHARD, 128), F32)
            for i in range(3):
                stage[0, i : i + 1, 0:SHARD] = vec_ref[i, 0:1]
                stage[0, 3 + i : 4 + i, 0:SHARD] = vec_ref[i, 1:2]
            stage[1, :, 0:SHARD] = stage[0, :, 0:128].T[0:SHARD]
            vslab[x, core, z, y] = stage[1, :, 0:128].astype(BF16)
            greet(place, along_dp=True)
            gather.start(0, 0)
            gather.start(1, 0)
            pack(1)
            spots = lax.broadcasted_iota(jnp.int32, (CLS_PAD, CLS_DEV), 0)
            wanted = order_ref[...]
            for s in range(8):
                dest = lax.rem(place.dp + s, 8)
                hit = jnp.logical_and(wanted == spots + dest * CLS_DEV, spots < CLS_DEV)
                hit = jnp.where(hit, 1.0, 0.0).astype(BF16)
                out_cls[s] = dot(hit, cot_ref[0, 0]).astype(BF16)
            gather.step(0, 0)
            gather.step(1, 0)
            gather.start(2, 0)
            gather.start(3, 0)
            v0_ref[...] = jnp.zeros_like(v0_ref)
            v1_ref[...] = jnp.zeros_like(v1_ref)
            wide[TOK_DEV:] = jnp.zeros((WIDE - TOK_DEV, D), F32)
            tile_rows(0, rows_s)
            for at in blocks(ROWS, SUB):
                h1_s[at, :] = normalise(rows_s[at, :].astype(F32))[0]
            gather.step(0, 1)
            gather.step(1, 1)
            gather.step(2, 0)
            gather.step(3, 0)
            for index in range(PACKS + 1, 2 * PACKS + 1):
                gather.start(index, 0)
            tile_rows(1, cot_s)
            gather.wait(0, 2)
            for f in range(4):
                rows = vslab[f // 2, f % 2].reshape(D, 128).astype(F32).T
                for block, v_ref in enumerate((v0_ref, v1_ref)):
                    v_ref[3 * f : 3 * f + 3, :] = rows[block * 3 : block * 3 + 3, :]
            land(1)

        def at_step(turn, *actions):
            @pl.when(step == turn)
            def _():
                for action, *args in actions:
                    action(*args)

        at_step(attend_first + 1, (gather.step, 2, 1), (gather.step, 3, 1), (gather.step, 4, 0))
        at_step(attend_first + 2, (gather.step, 5, 0))
        at_step(attend_first + 3, (gather.step, 2, 2), (gather.step, 3, 2), (gather.step, 4, 1), (gather.step, 6, 0))

        @pl.when(jnp.logical_and(step >= attend_first, step < expand_first))
        def _():
            here = pl.ds(pl.multiple_of((step - attend_first) * CHUNK, CHUNK), CHUNK)

            def put_mid(at, h1, a2):
                h1_ref[at, :] = h1
                a2_ref[at, :] = a2
                h1_s.at[here][at, :] = h1
                a2_s.at[here][at, :] = a2

            saved = (a1_ref, qkvo_ref, pt_ref, o_ref)
            attend_chunk(
                rows_s.at[here], bias_ref, (wq.at[0], wp.at[0]), v0_ref, saved, score_s, put_mid, h1_s.at[here]
            )

        @pl.when(step == expand_first)
        def _():
            for copy in cls:
                copy.start()
            land(2)
            land(3)
            gather.step(5, 1)

        at_step(expand_first + 1, (gather.step, 4, 2), (gather.step, 6, 1))
        at_step(expand_first + 2, (gather.step, 5, 2), (gather.step, 6, 2))
        at_step(expand_first + 3, (land, 4), (land, 5))

        @pl.when(step >= expand_first)
        def _():
            here = pl.ds(pl.multiple_of((step - expand_first) * CHUNK, CHUNK), CHUNK)

            def finish(at, rows):
                mid_ref[at, :] = rows

            expand_chunk(h1_s.at[here], a2_s.at[here], (w1.at[0], w2.at[0]), v0_ref, (u_ref, gp_ref), finish)

        @pl.when(step == last)
        def _():
            for copy in cls:
                copy.wait_recv()
            total = out_cls[0].astype(F32)
            for s in range(7):
                total = total + in_cls[s].astype(F32)
            ret_ref[...] = total.astype(BF16)
            land(6)
            for copy in cls:
                copy.wait_send()
            gather.drain()
            for store in stores + keeps[0] + keeps[1]:
                store.wait()

    vmem = pl.BlockSpec(memory_space=pltpu.VMEM)
    there = pl.BlockSpec(memory_space=pl.ANY)
    early = [
        ((ROWS, D), BF16, CHUNK),
        ((ROWS, 3 * D), BF16, CHUNK),
        ((TILES * HEADS, TILE, TILE), BF16, PER_STEP * HEADS),
        ((ROWS, D), BF16, CHUNK),
        ((ROWS, D), F32, CHUNK),
        ((ROWS, D), BF16, CHUNK),
    ]
    late = [((ROWS, FF), BF16, CHUNK), ((ROWS, FF), BF16, CHUNK)]
    shapes = [((ROWS, D), F32, late_block((CHUNK, D), expand_first))]
    shapes += [(shape, dtype, late_block((size, *shape[1:]), attend_first)) for shape, dtype, size in early]
    shapes += [(shape, dtype, late_block((size, *shape[1:]), expand_first)) for shape, dtype, size in late]
    shapes += [((16, D), F32, whole((16, D)))] * 2 + [((CLS_PAD, D), BF16, whole((CLS_PAD, D)))]
    forms = ((3 * D, D), (D, D), (D, FF), (D, FF))
    shapes += [((ROWS, D), BF16, there)] * 2 + [(form, BF16, there) for form in forms * 2]
    outs = pl.pallas_call(
        kernel,
        grid=(last + 1,),
        in_specs=[whole(a.shape) for a in (qkv, proj, fc1, fc2, vec, order, cot)]
        + [
            pl.BlockSpec(
                (1, TILE, TILE),
                lambda i: ((jnp.clip(i - attend_first, 0, STEPS - 1) * PER_STEP) // VIEWS, 0, 0),
            ),
            there,
            there,
        ],
        out_specs=[spec for _, _, spec in shapes],
        out_shape=[jax.ShapeDtypeStruct(shape, dtype) for shape, dtype, _ in shapes],
        scratch_shapes=[
            pltpu.VMEM((2 * PACKS, *GATHERED), BF16),
            pltpu.VMEM((2, 2, 4, 2, SHARD, 128), BF16),
            *[pltpu.VMEM((2, *form), BF16) for form in forms],
            pltpu.VMEM((2, SHARD, D), F32),
            pltpu.VMEM((8, CLS_PAD, D), BF16),
            pltpu.VMEM((7, CLS_PAD, D), BF16),
            pltpu.VMEM((2, TOK_DEV, D), BF16),
            pltpu.VMEM((WIDE, D), F32),
            pltpu.VMEM((ROWS, D), BF16),
            pltpu.VMEM((ROWS, D), BF16),
            pltpu.VMEM((ROWS, D), F32),
            pltpu.VMEM((ROWS, D), BF16),
            SPARE[0],
            pltpu.SemaphoreType.DMA((2 * PACKS, 8)),
            pltpu.SemaphoreType.DMA((2 * PACKS, 8)),
            pltpu.SemaphoreType.DMA((8,)),
            pltpu.SemaphoreType.DMA((8,)),
            pltpu.SemaphoreType.DMA((7,)),
            pltpu.SemaphoreType.DMA((7,)),
            pltpu.SemaphoreType.DMA((4,)),
            pltpu.SemaphoreType.DMA((2, 4)),
        ],
        compiler_params=pltpu.CompilerParams(
            dimension_semantics=("arbitrary",), collective_id=0, has_side_effects=True, vmem_limit_bytes=VMEM_LIMIT
        ),
        name="gather_forward",
    )(qkv, proj, fc1, fc2, vec, order, cot, bias, tokens, out_cot)
    middle, saved, vecs, returned = outs[0], outs[1:9], outs[9:11], outs[11]
    return middle, saved, vecs, returned, outs[12], outs[13], outs[14:18], outs[18:22]


class Scatter:
    def __init__(self, place, source, sum1, in1, sum2, in2, in3, send, recv):
        self.place, self.source = place, source
        self.sum1, self.in1, self.sum2, self.in2, self.in3 = sum1, in1, sum2, in2, in3
        self.send, self.recv = send, recv

    def copies(self, c, phase):
        place, send, recv = self.place, self.send, self.recv
        if phase == 0:
            mine = self.source.at[c, :, 1 - place.core]
            return [remote(mine, self.in1.at[c], send.at[c, 0], recv.at[c, 0], place.sibling())]
        if phase == 1:
            out = []
            for s in (1, 2, 3):
                px, py = place.plane_spot(s)
                mine = self.sum1.at[c, px, :, py]
                out.append(remote(mine, self.in2.at[c, s - 1], send.at[c, s], recv.at[c, s], place.in_plane(s)))
            return out
        out = []
        for s in (1, 2, 3):
            mine = self.sum2.at[c, lax.rem(place.z + s, 4)]
            out.append(remote(mine, self.in3.at[c, s - 1], send.at[c, 3 + s], recv.at[c, 3 + s], place.along_z(s)))
        return out

    def start(self, c, phase):
        for copy in self.copies(c, phase):
            copy.start()

    def wait(self, c, phase):
        for copy in self.copies(c, phase):
            copy.wait_recv()

    def plane(self, c):
        self.wait(c, 0)
        for px in range(2):
            total = self.source[c, px, self.place.core].astype(F32) + self.in1[c, px].astype(F32)
            self.sum1[c, px] = total.astype(BF16)
        self.start(c, 1)

    def line(self, c):
        self.wait(c, 1)
        total = self.sum1[c, self.place.x, :, self.place.y].astype(F32)
        for s in range(3):
            total = total + self.in2[c, s].astype(F32)
        self.sum2[c] = total.astype(BF16)
        self.start(c, 2)

    def total(self, c):
        self.wait(c, 2)
        total = self.sum2[c, self.place.z].astype(F32)
        for s in range(3):
            total = total + self.in3[c, s].astype(F32)
        return total

    def drain(self, kinds):
        for c in range(kinds):
            for phase in range(3):
                for copy in self.copies(c, phase):
                    copy.wait_send()


SCATTER_SCRATCH = [
    pltpu.VMEM((PACKS, 2, 4, 2, SHARD, D), BF16),
    pltpu.VMEM((PACKS, 2, 4, 2, SHARD, D), BF16),
    pltpu.VMEM((PACKS, 4, SHARD, D), BF16),
    pltpu.VMEM((PACKS, 3, 4, SHARD, D), BF16),
    pltpu.VMEM((PACKS, 3, SHARD, D), BF16),
    pltpu.SemaphoreType.DMA((PACKS, 7)),
    pltpu.SemaphoreType.DMA((PACKS, 7)),
]


def backward_scatter(dy, rows, saved, weights, vec, other, vg_other, cls_rows):
    middle, attend_first = STEPS, STEPS + 1
    turn_back, input_first = 2 * STEPS + 1, 2 * STEPS + 2
    last = 3 * STEPS + 1

    def kernel(
        dy_ref, x_ref, a1_hbm, qkv_ref, pt_ref, o_ref, h1_ref, a2_hbm, u_hbm, gp_ref, wq, wp, w1, w2, vec_ref,
        other_ref, vhi_ref, cls_ref,
        dx_ref, low_ref, high_ref, vsum_ref, cls_out,
        a2_s, u_s, dy_s, dz_s, dh_s, dol_s, turned, keep_s, dx_s, slab_s, vg_s, load_sem, score_s, ds_s, *refs,
    ):
        high_refs, low_refs, (vin, vacc, cls_all, vsend, vrecv, csend, crecv) = refs[0:7], refs[7:14], refs[14:]
        step = pl.program_id(0)
        place = Place()
        high = Scatter(place, other_ref, *high_refs)
        low = Scatter(place, slab_s, *low_refs)
        o_s, a1_s, dl_s = u_s.at[:, 0:D], u_s.at[:, D : 2 * D], dz_s.at[:, 0 : 3 * D]
        moves = ((a2_hbm, a2_s), (u_hbm, u_s), (a1_hbm, a1_s))
        loads = [pltpu.make_async_copy(there, mine, load_sem.at[i]) for i, (there, mine) in enumerate(moves)]
        cls = [
            remote(cls_ref, cls_all.at[place.dp], csend.at[s - 1], crecv.at[s - 1], place.along_dp(s))
            for s in range(1, 8)
        ]
        vec = [remote(vacc.at[0], vin.at[0], vsend.at[0], vrecv.at[0], place.sibling())]
        vec += [
            remote(vacc.at[1], vin.at[s], vsend.at[s], vrecv.at[s], place.in_plane(s)) for s in (1, 2, 3)
        ]
        vec += [
            remote(vacc.at[2], vin.at[3 + s], vsend.at[3 + s], vrecv.at[3 + s], place.along_z(s)) for s in (1, 2, 3)
        ]

        def at_step(turn, *actions):
            @pl.when(step == turn)
            def _():
                for action, *args in actions:
                    action(*args)

        @pl.when(step == 0)
        def _():
            vg_s[...] = jnp.zeros_like(vg_s)
            loads[0].start()
            loads[1].start()
            greet(place, along_dp=True)
            for c in range(PACKS):
                high.start(c, 0)
            cls_all[place.dp] = cls_ref[...]
            for copy in cls:
                copy.start()

        at_step(2, (high.plane, 2), (high.plane, 1), (high.plane, 0))

        @pl.when(step < middle)
        def _():
            here = pl.ds(pl.multiple_of(step * CHUNK, CHUNK), CHUNK)
            grads = (dy_s.at[here], dz_s.at[here], dh_s.at[here], dol_s.at[here], keep_s.at[here])
            expand_back(lambda at: dy_ref[at, :], (wp, w1, w2), vec_ref, (h1_ref, gp_ref), grads, vg_s)

        @pl.when(step == middle)
        def _():
            loads[0].wait()
            loads[1].wait()
            down_grads(dy_s, u_s, turned, slab_s)
            low.start(2, 0)
            loads[2].start()
            up_grads(a2_s, dz_s, turned, slab_s, vg_s)
            low.start(1, 0)

        at_step(attend_first, (high.line, 2))
        at_step(attend_first + 1, (high.line, 1), (low.plane, 2))
        at_step(attend_first + 2, (low.plane, 1))
        at_step(attend_first + 3, (high.line, 0))

        @pl.when(jnp.logical_and(step >= attend_first, step < turn_back))
        def _():
            turn = step - attend_first
            here = pl.ds(pl.multiple_of(turn * CHUNK, CHUNK), CHUNK)

            o_s.at[here][...] = o_ref[...]
            attend_back((qkv_ref, pt_ref, o_ref), (dol_s.at[here], dl_s.at[here]), (score_s, ds_s))

        @pl.when(step == turn_back)
        def _():
            loads[2].wait()
            attention_grads(a1_s, dl_s, o_s, dh_s, turned, slab_s, vg_s)
            low.start(0, 0)

        at_step(input_first + 1, (low.line, 2))
        at_step(input_first + 3, (low.plane, 0))

        @pl.when(step >= input_first)
        def _():
            turn = step - input_first
            here = pl.ds(pl.multiple_of(turn * CHUNK, CHUNK), CHUNK)

            def dx_put(at, rows):
                dx_s[at, :] = rows

            input_back(x_ref, wq, vec_ref, (dl_s.at[here], keep_s.at[here]), vg_s, dx_put)
            untile(turn, dx_s, dx_ref)

        @pl.when(step == last)
        def _():
            vacc[0, 0:16] = vg_s[...]
            vacc[0, 16:32] = vhi_ref[...]
            vec[0].start()
            low.line(1)
            for c in range(PACKS):
                high_ref[c] = high.total(c)
            vec[0].wait_recv()
            vacc[1] = vacc[0] + vin[0]
            for copy in vec[1:4]:
                copy.start()
            low_ref[2] = low.total(2)
            for copy in cls:
                copy.wait_recv()
            cls_out[...] = cls_all[...]
            for copy in vec[1:4]:
                copy.wait_recv()
            vacc[2] = vacc[1] + vin[1] + vin[2] + vin[3]
            for copy in vec[4:7]:
                copy.start()
            low.line(0)
            low_ref[1] = low.total(1)
            for copy in vec[4:7]:
                copy.wait_recv()
            vsum_ref[...] = vacc[2] + vin[4] + vin[5] + vin[6]
            low_ref[0] = low.total(0)
            for copy in cls + vec:
                copy.wait_send()
            high.drain(PACKS)
            low.drain(PACKS)

    there = pl.BlockSpec(memory_space=pl.ANY)

    def early(width):
        return late_block((CHUNK, width), 0)

    def late(width):
        return late_block((CHUNK, width), attend_first)

    out_shapes = [
        ((TOK_DEV, D), F32),
        ((PACKS, SHARD, D), F32),
        ((PACKS, SHARD, D), F32),
        ((32, D), F32),
        ((8, CLS_PAD, D), BF16),
    ]
    return pl.pallas_call(
        kernel,
        grid=(last + 1,),
        in_specs=[
            early(D),
            late_block((CHUNK, D), input_first),
            there,
            late(3 * D),
            late_block((PER_STEP * HEADS, TILE, TILE), attend_first),
            late(D),
            early(D),
            there,
            there,
            early(FF),
        ]
        + WEIGHT_SPECS
        + [whole(SPLIT), whole((16, D)), whole((CLS_PAD, D))],
        out_specs=[whole(shape) for shape, _ in out_shapes],
        out_shape=[jax.ShapeDtypeStruct(shape, dtype) for shape, dtype in out_shapes],
        scratch_shapes=[
            pltpu.VMEM((ROWS, D), BF16),
            pltpu.VMEM((ROWS, FF), BF16),
            pltpu.VMEM((ROWS, D), BF16),
            pltpu.VMEM((ROWS, FF), BF16),
            pltpu.VMEM((ROWS, D), BF16),
            pltpu.VMEM((ROWS, D), BF16),
            pltpu.VMEM((D + ONES, ROWS), BF16),
            pltpu.VMEM((ROWS, D), F32),
            pltpu.VMEM((CHUNK, D), F32),
            pltpu.VMEM(SPLIT, BF16),
            pltpu.VMEM((16, D), F32),
            pltpu.SemaphoreType.DMA((4,)),
        ]
        + SPARE
        + SCATTER_SCRATCH * 2
        + [
            pltpu.VMEM((7, 32, D), F32),
            pltpu.VMEM((3, 32, D), F32),
            pltpu.VMEM((8, CLS_PAD, D), BF16),
            pltpu.SemaphoreType.DMA((7,)),
            pltpu.SemaphoreType.DMA((7,)),
            pltpu.SemaphoreType.DMA((7,)),
            pltpu.SemaphoreType.DMA((7,)),
        ],
        compiler_params=pltpu.CompilerParams(
            dimension_semantics=("arbitrary",), collective_id=1, has_side_effects=True, vmem_limit_bytes=VMEM_LIMIT
        ),
        name="backward_scatter",
    )(dy, rows, *saved, *weights, vec, other, vg_other, cls_rows)


def apply_updates(low, high, vec_sum, cls_all, order, state, vec_state):
    def kernel(low_ref, high_ref, vsum_ref, cls_ref, order_ref, *rest):
        state, vecs, outs, vec_outs = rest[0:12], rest[12:15], rest[15:27], rest[27:30]
        regroup_ref = rest[30]

        def update(kind, block, grad):
            w_ref, m_ref, s_ref = state[kind], state[4 + kind], state[8 + kind]
            new = adamw(w_ref[block], m_ref[block], s_ref[block], grad, 1.0, step_rate)
            for slot in range(3):
                outs[slot * 4 + kind][block] = new[slot]

        for block, grad_ref in enumerate((low_ref, high_ref)):
            total = grad_ref[0]
            update(0, block, total[:, 0:288])
            update(1, block, pltpu.roll(total, 96, 1)[:, 0:96])
            update(2, block, grad_ref[1])
            total = grad_ref[2]
            both = jnp.concatenate([total[:, 0:192], pltpu.roll(total, 192, 1)[:, 0:192]], axis=0)
            update(3, block, both.T)
        dp, fsdp = lax.axis_index("dp"), lax.axis_index("fsdp")
        mine = pltpu.roll(vsum_ref[...], lax.rem(D - dp * SHARD, D), 1)
        mine = pltpu.roll(mine, lax.rem(32 - 3 * fsdp, 32), 0)
        for column in range(3):
            grad = jnp.concatenate([mine[16 * b + column : 16 * b + column + 1, 0:SHARD] for b in range(2)], axis=0)
            new = adamw(vecs[0][column], vecs[1][column], vecs[2][column], grad, 0.0, vector_rate)
            for slot in range(3):
                vec_outs[slot][column] = new[slot]
        spots = lax.broadcasted_iota(jnp.int32, (8 * CLS_PAD, CLS_DEV), 0)
        code = (spots // CLS_PAD) * CLS_DEV + spots % CLS_PAD
        hit = jnp.logical_and(order_ref[...] == code, spots % CLS_PAD < CLS_DEV)
        hit = jnp.where(hit, 1.0, 0.0).astype(BF16)
        regrouped = lax.dot_general(
            hit, cls_ref[...].reshape(8 * CLS_PAD, D), (((0,), (0,)), ((), ())), preferred_element_type=F32
        )
        regroup_ref[0, 0] = regrouped.astype(BF16)

    out_shape = [jax.ShapeDtypeStruct(a.shape, F32) for a in (*state, *vec_state)]
    out_shape.append(jax.ShapeDtypeStruct((1, 1, CLS_DEV, D), BF16))
    vmem = pl.BlockSpec(memory_space=pltpu.VMEM)
    return pl.pallas_call(
        kernel,
        out_shape=out_shape,
        in_specs=[vmem] * 20,
        out_specs=[vmem] * 16,
        compiler_params=pltpu.CompilerParams(vmem_limit_bytes=VMEM_LIMIT),
        name="apply_updates",
    )(low, high, vec_sum, cls_all, order, *state, *vec_state)


def tile_rows(rows):
    edge = VIEWS * GLOB_TOK
    glob = rows[:edge].reshape(VIEWS, GLOB_TOK, D)
    crop = rows[edge:].reshape(GROUPS, CROP_GROUP * CROP_TOK, D)
    glob = jnp.pad(glob, ((0, 0), (0, TILE - GLOB_TOK), (0, 0)))
    crop = jnp.pad(crop, ((0, 0), (0, TILE - CROP_GROUP * CROP_TOK), (0, 0)))
    return jnp.concatenate([glob, crop], axis=0).reshape(ROWS, D)


def mask_bias():
    row = np.arange(TILE)
    glob = row // GLOB_TOK
    crop = np.minimum(row // CROP_TOK, CROP_GROUP)
    same = np.stack([group[:, None] == group[None, :] for group in (glob, crop)])
    return np.where(same, 0.0, -1e30).astype(np.float32)


def local_fast(
    tokens, focal_count, cls_order, out_cotangent, cls_cotangent,
    qkv_weight, proj_weight, fc1_weight, fc2_weight, vec_params,
    qkv_first, proj_first, fc1_first, fc2_first, vec_first,
    qkv_second, proj_second, fc1_second, fc2_second, vec_second,
):
    def turn(narrow):
        return narrow.transpose(2, 0, 1)

    bias = jnp.asarray(mask_bias())
    middle, saved, vec, returned, rows, cotangent, lower, upper = gather_forward(
        qkv_weight, proj_weight, fc1_weight, fc2_weight, turn(vec_params),
        cls_order, cls_cotangent, tokens, out_cotangent, bias,
    )
    shown, cls_rows, middle_grad, slab_hi, vg_hi = second_block(
        middle, bias, upper, vec[1], cotangent, returned, focal_count
    )
    input_grad, low, high, vec_sum, cls_all = backward_scatter(
        middle_grad, rows, saved, lower, vec[0], slab_hi, vg_hi, cls_rows
    )
    state = (
        qkv_weight, proj_weight, fc1_weight, fc2_weight,
        qkv_first, proj_first, fc1_first, fc2_first,
        qkv_second, proj_second, fc1_second, fc2_second,
    )
    vec_state = (turn(vec_params), turn(vec_first), turn(vec_second))
    out = apply_updates(low, high, vec_sum, cls_all, cls_order, state, vec_state)
    return (
        shown[None, None],
        out[15],
        input_grad[None, None],
        *out[0:4], out[12].transpose(1, 2, 0),
        *out[4:8], out[13].transpose(1, 2, 0),
        *out[8:12], out[14].transpose(1, 2, 0),
    )


def local_any(
    tokens, focal_count, cls_order, out_cotangent, cls_cotangent,
    qkv_weight, proj_weight, fc1_weight, fc2_weight, vec_params,
    qkv_first, proj_first, fc1_first, fc2_first, vec_first,
    qkv_second, proj_second, fc1_second, fc2_second, vec_second,
):
    def gather(shard):
        wide = lax.all_gather(shard.astype(BF16), "fsdp", axis=2, tiled=True)
        return lax.all_gather(wide, "dp", axis=1, tiled=True)

    params = (qkv_weight, proj_weight, fc1_weight, fc2_weight, vec_params)
    qkv, proj, fc1, fc2, vectors = (gather(param) for param in params)
    blocks = [(qkv[b].T, proj[b].T, fc1[b], fc2[b].T) for b in range(2)]
    vec = jnp.pad(vectors.astype(F32).transpose(0, 2, 1), ((0, 0), (0, 4), (0, 0)))
    dp, fsdp = lax.axis_index("dp"), lax.axis_index("fsdp")
    total_cls = lax.axis_size("dp") * CLS_DEV
    picker = (cls_order[0][:, None] == jnp.arange(total_cls, dtype=jnp.int32)[None, :]).astype(BF16)
    spread = lax.dot_general(
        picker, cls_cotangent[0, 0], (((0,), (0,)), ((), ())), preferred_element_type=F32
    )
    returned = lax.psum_scatter(spread, "dp", scatter_dimension=0, tiled=True).astype(BF16)
    returned = jnp.pad(returned, ((0, CLS_PAD - CLS_DEV), (0, 0)))
    bias = jnp.asarray(mask_bias())
    rows = tile_rows(tokens[0, 0])
    middle, saved = first_forward(rows, bias, blocks[0], vec[0])
    shown, cls_rows, middle_grad, slab_hi, vg_hi = second_block(
        middle, bias, blocks[1], vec[1], tile_rows(out_cotangent[0, 0]), returned, focal_count
    )
    input_grad, slab_lo, vg_lo = first_backward(middle_grad, rows, saved, blocks[0], vec[0])
    slabs, vg = (slab_lo, slab_hi), (vg_lo, vg_hi)
    pooled = lax.all_gather(cls_rows[:CLS_DEV], "dp", axis=0, tiled=True)
    regrouped = jnp.dot(picker, pooled, preferred_element_type=F32).astype(BF16)

    def scatter(full):
        rows = lax.psum_scatter(full, "dp", scatter_dimension=1, tiled=True)
        return lax.psum_scatter(rows, "fsdp", scatter_dimension=2, tiled=True)

    packs = jnp.stack(slabs).reshape(2, PACKS, 4, D, D).astype(F32)
    qkv_full = packs[:, 0, :, :, 0:288].transpose(0, 2, 1, 3).reshape(2, D, 3 * D)
    proj_full = packs[:, 0, :, :, 288:384].transpose(0, 2, 1, 3).reshape(2, D, D)
    fc1_full = packs[:, 1].transpose(0, 2, 1, 3).reshape(2, D, FF)
    turned = packs[:, 2].reshape(2, 4, 8, SHARD, 2, 192)
    fc2_full = turned.transpose(0, 2, 5, 1, 4, 3).reshape(2, FF, D)
    vec_full = jnp.stack(vg)[:, :12].transpose(0, 2, 1)
    owned = [scatter(full) for full in (qkv_full, proj_full, fc1_full, fc2_full, vec_full)]
    firsts = (qkv_first, proj_first, fc1_first, fc2_first, vec_first)
    seconds = (qkv_second, proj_second, fc1_second, fc2_second, vec_second)
    flags = (1.0, 1.0, 1.0, 1.0, 0.0)
    rates = (step_rate,) * 4 + (vector_rate,)
    new = [adamw(*args) for args in zip(params, firsts, seconds, owned, flags, rates)]
    return (
        shown[None, None],
        regrouped[None, None],
        input_grad[None, None],
        *(item[0] for item in new),
        *(item[1] for item in new),
        *(item[2] for item in new),
    )


def solution(mesh):
    sizes = dict(mesh.shape)
    local = local_fast if (sizes["dp"], sizes["fsdp"]) == (8, 4) else local_any
    weight = P(None, "dp", "fsdp")
    rows = P("dp", "fsdp", None, None)
    return jax.shard_map(
        local,
        mesh=mesh,
        in_specs=(rows, P("dp", "fsdp"), P("fsdp", "dp"), rows, rows) + (weight,) * 15,
        out_specs=(rows, rows, rows) + (weight,) * 15,
        check_vma=False,
    )
```
